32 devices in a mesh: grp: 2 (over y), gy: 4 (over z), gz: 2 (over x), vert: 2 (over core).
Axes of the slice: x: 2, y: 2, z: 4, core: 2. Of those that a mesh axis runs over, the one named last changes fastest.
Arguments:
- field: float32 [16, 64, 64, 512], P(('grp', 'vert'), 'gy', 'gz'), parts along dimension 0, as said below
- omega_x: float32 [512, 128], replicated, may hold values from -6 to 6
- omega_y: float32 [64, 32], replicated, may hold values from -6 to 6
- rank_x: int32 [2], P('grp'), parts along dimension 0, may hold values from 64 to 128
- rank_y: int32 [2], P('grp'), parts along dimension 0, may hold values from 16 to 32
Outputs:
- core: float32 [16, 32, 64, 128], P(('grp', 'vert'), 'gy', 'gz'), parts along dimension 0
- factor_x: float32 [1024, 128], P('grp'), parts along dimension 0
- factor_y: float32 [128, 32], P('grp'), parts along dimension 0
The draws below stay inside these ranges and needn't reach their ends.
There are 2 independent parts, one for each index of `grp`. The reference program is written for one: setup_inputs(seed, part) draws one part's arguments, and reference() takes and returns one part's arrays. A program takes and returns all parts, laid end to end along the dimension named above; an argument that names none is the same for every part. Nothing has to cross between parts.
Inputs may be any that keep to these rules, and one draw needn't show every extreme that they name: field values are finite and of order one; their spread differs between cells of the first dimension.
All inputs are finite; a program needn't handle non-finite values.
Results may differ from the reference program's by a relative error of at most 0.000086.
Values sent between devices are 32-bit elements; how exact they have to be, the bound alone decides.
A program may use at most 64 MiB of HBM per device.

```python
import jax
import jax.numpy as jnp
from jax import lax

X = 512
V = 8
RX = 128
RY = 32
Y = 64
Z = 64


def draw_field(key, part):
    key_base, key_cols, key_rows, key_planes = jax.random.split(jax.random.fold_in(key, 7), 4)
    base = jax.random.normal(key_base, (V, Y, Z, X), jnp.float32)
    column_scale = jnp.exp(jax.random.uniform(key_cols, (X,), jnp.float32, 0.0, 1.39))
    row_scale = jnp.exp(jax.random.uniform(key_rows, (Y,), jnp.float32, -0.6, 0.6))
    plane_scale = jnp.exp(jax.random.uniform(key_planes, (V,), jnp.float32, -0.5, 0.5))
    return base * column_scale[None, None, None, :] * row_scale[None, :, None, None] * plane_scale[:, None, None, None]


def centred(key, dims, width, most, held_as=jnp.bfloat16):
    entries = width * jax.random.normal(key, dims, jnp.float32)
    return jnp.clip(entries, min=-most, max=most).astype(held_as)


def setup_inputs(seed: int = 0, part: int = 0) -> dict:
    seeds = jax.random.split(jax.random.key(seed), 6)
    part_splits = jax.random.split(jax.random.fold_in(seeds[5], part), 6)
    field = draw_field(jax.random.fold_in(jax.random.fold_in(seeds[5], part), 71), part)
    omega_x = centred(seeds[1], (X, RX), 1.0, 6.0, jnp.float32)
    omega_y = centred(seeds[2], (Y, RY), 1.0, 6.0, jnp.float32)
    rank_x = jax.random.randint(part_splits[3], (1,), RX // 2, RX + 1).astype(jnp.int32)
    rank_y = jax.random.randint(part_splits[4], (1,), RY // 2, RY + 1).astype(jnp.int32)
    return dict(field=field, omega_x=omega_x, omega_y=omega_y, rank_x=rank_x, rank_y=rank_y)


def orthonormal(sketch, trunc_rank):
    precise = lax.Precision.HIGHEST
    small_gram = jnp.dot(sketch.T, sketch, precision=precise)
    lower_factor = jnp.linalg.cholesky(small_gram)
    basis = lax.linalg.triangular_solve(lower_factor, sketch, left_side=False, lower=True, transpose_a=True)
    column_ids = jnp.arange(sketch.shape[1], dtype=jnp.int32)
    kept = (column_ids < trunc_rank[0]).astype(jnp.float32)
    return basis * kept[None, :]

def reference(field, omega_x, omega_y, rank_x, rank_y):
    precise = lax.Precision.HIGHEST
    flat = field.reshape(-1, X)
    gram_x = jnp.dot(flat.T, flat, precision=precise) / float(V * Y * Z)
    sketch_x = jnp.dot(gram_x, omega_x, precision=precise)
    factor_x = orthonormal(sketch_x, rank_x)
    core_x = jnp.dot(flat, factor_x, precision=precise).reshape(V, Y, Z, RX)
    gram_y = jnp.einsum('vazr,vbzr->ab', core_x, core_x, precision=precise) / float(V * Z * RX)
    sketch_y = jnp.dot(gram_y, omega_y, precision=precise)
    factor_y = orthonormal(sketch_y, rank_y)
    core = jnp.einsum('vyzr,yk->vkzr', core_x, factor_y, precision=precise)
    return (core, factor_x, factor_y)
```

```python
import jax
import jax.numpy as jnp
from jax import lax
from jax.sharding import PartitionSpec as P

HIGHEST = lax.Precision.HIGHEST


def inverse_factor(sketch):
    small_gram = jnp.dot(sketch.T, sketch, precision=HIGHEST)
    lower = jnp.linalg.cholesky(small_gram)
    eye = jnp.eye(lower.shape[0], dtype=jnp.float32)
    return lax.linalg.triangular_solve(lower, eye, left_side=True, lower=True)


def plain_body(field, omega_x, omega_y, rank_x, rank_y):
    planes, rows_y, rows_z, cells_x = field.shape
    all_planes = planes * lax.axis_size("vert")
    all_rows_y = rows_y * lax.axis_size("gy")
    all_rows_z = rows_z * lax.axis_size("gz")
    flat = field.reshape(-1, cells_x)
    proj = jnp.dot(flat, omega_x, precision=HIGHEST)
    local_sketch = jnp.dot(flat.T, proj, precision=HIGHEST)
    sketch_x = lax.psum(local_sketch, ("gy", "gz", "vert")) / float(all_planes * all_rows_y * all_rows_z)
    ranks_x = sketch_x.shape[1]
    terms = jnp.dot(flat, sketch_x, precision=HIGHEST).reshape(planes, rows_y, rows_z, ranks_x)
    spread = lax.all_to_all(terms, "gy", split_axis=2, concat_axis=1, tiled=True)
    inv_x = inverse_factor(sketch_x)
    kept_x = (jnp.arange(ranks_x) < rank_x[0]).astype(jnp.float32)
    inv_x = inv_x * kept_x[:, None]
    factor_x = jnp.dot(sketch_x, inv_x.T, precision=HIGHEST)
    core_x = jnp.einsum("vyzr,sr->vyzs", spread, inv_x, precision=HIGHEST)
    divisor_y = float(all_planes * all_rows_z * ranks_x)
    local_gram_y = jnp.einsum("vazr,vbzr->ab", core_x, core_x, precision=HIGHEST)
    sketch_y = lax.psum(jnp.dot(local_gram_y, omega_y, precision=HIGHEST), ("gy", "gz", "vert")) / divisor_y
    inv_y = inverse_factor(sketch_y)
    kept_y = (jnp.arange(inv_y.shape[0]) < rank_y[0]).astype(jnp.float32)
    factor_y = jnp.dot(sketch_y, (inv_y * kept_y[:, None]).T, precision=HIGHEST)
    mine = jnp.einsum("vyzr,yk->vkzr", core_x, factor_y, precision=HIGHEST)
    core = lax.all_to_all(mine, "gy", split_axis=1, concat_axis=2, tiled=True)
    return (core, factor_x, factor_y)


def solution(mesh):
    in_specs = (P(("grp", "vert"), "gy", "gz", None), P(), P(), P("grp"), P("grp"))
    out_specs = (P(("grp", "vert"), "gy", "gz", None), P("grp", None), P("grp", None))
    return jax.shard_map(plain_body, mesh=mesh, in_specs=in_specs, out_specs=out_specs, check_vma=False)
```

```python
import functools

import jax
import jax.numpy as jnp
from jax import lax
from jax.experimental import pallas as pl
from jax.experimental.pallas import tpu as pltpu
from jax.sharding import PartitionSpec as P

HIGHEST = lax.Precision.HIGHEST


def inverse_factor(sketch):
    small_gram = jnp.dot(sketch.T, sketch, precision=HIGHEST)
    lower = jnp.linalg.cholesky(small_gram)
    eye = jnp.eye(lower.shape[0], dtype=jnp.float32)
    return lax.linalg.triangular_solve(lower, eye, left_side=True, lower=True)


def plain_body(field, omega_x, omega_y, rank_x, rank_y):
    planes, rows_y, rows_z, cells_x = field.shape
    all_planes = planes * lax.axis_size("vert")
    all_rows_y = rows_y * lax.axis_size("gy")
    all_rows_z = rows_z * lax.axis_size("gz")
    flat = field.reshape(-1, cells_x)
    proj = jnp.dot(flat, omega_x, precision=HIGHEST)
    local_sketch = jnp.dot(flat.T, proj, precision=HIGHEST)
    sketch_x = lax.psum(local_sketch, ("gy", "gz", "vert")) / float(all_planes * all_rows_y * all_rows_z)
    ranks_x = sketch_x.shape[1]
    terms = jnp.dot(flat, sketch_x, precision=HIGHEST).reshape(planes, rows_y, rows_z, ranks_x)
    spread = lax.all_to_all(terms, "gy", split_axis=2, concat_axis=1, tiled=True)
    inv_x = inverse_factor(sketch_x)
    kept_x = (jnp.arange(ranks_x) < rank_x[0]).astype(jnp.float32)
    inv_x = inv_x * kept_x[:, None]
    factor_x = jnp.dot(sketch_x, inv_x.T, precision=HIGHEST)
    core_x = jnp.einsum("vyzr,sr->vyzs", spread, inv_x, precision=HIGHEST)
    divisor_y = float(all_planes * all_rows_z * ranks_x)
    local_gram_y = jnp.einsum("vazr,vbzr->ab", core_x, core_x, precision=HIGHEST)
    sketch_y = lax.psum(jnp.dot(local_gram_y, omega_y, precision=HIGHEST), ("gy", "gz", "vert")) / divisor_y
    inv_y = inverse_factor(sketch_y)
    kept_y = (jnp.arange(inv_y.shape[0]) < rank_y[0]).astype(jnp.float32)
    factor_y = jnp.dot(sketch_y, (inv_y * kept_y[:, None]).T, precision=HIGHEST)
    mine = jnp.einsum("vyzr,yk->vkzr", core_x, factor_y, precision=HIGHEST)
    core = lax.all_to_all(mine, "gy", split_axis=1, concat_axis=2, tiled=True)
    return (core, factor_x, factor_y)


MESH = pl.DeviceIdType.MESH
NT = (((1,), (1,)), ((), ()))


def mm(a, b):
    return jnp.dot(a, b, precision=HIGHEST, preferred_element_type=jnp.float32)


def mm_nt(a, b):
    return lax.dot_general(a, b, NT, precision=HIGHEST, preferred_element_type=jnp.float32)


def eliminate(work, inv, size):
    rows = lax.broadcasted_iota(jnp.int32, (size, size), 0)
    cols = lax.broadcasted_iota(jnp.int32, (size, size), 1)
    inv[...] = (rows == cols).astype(jnp.float32)
    row_ids = lax.broadcasted_iota(jnp.int32, (size, 1), 0)
    lane_ids = lax.broadcasted_iota(jnp.int32, (1, size), 1)

    def step(j, pivots):
        full = work[...]
        row = work[pl.ds(j, 1), :]
        column = jnp.sum(jnp.where(cols == j, full, 0.0), axis=1, keepdims=True)
        pivot = jnp.sum(jnp.where(lane_ids == j, row, 0.0), axis=1, keepdims=True)
        factor = jnp.where(row_ids > j, column / pivot, 0.0)
        inv_row = inv[pl.ds(j, 1), :]
        work[...] = full - factor * row
        inv[...] = inv[...] - factor * inv_row
        return jnp.where(row_ids == j, pivot, pivots)

    pivots = lax.fori_loop(0, size, step, jnp.ones((size, 1), jnp.float32))
    inv[...] = inv[...] * lax.rsqrt(pivots)


def fused(dims, rank_x, rank_y, field, omega_x, omega_y_t, core_out, fx_out, fy_out,
          part, gathered, own_sum, sketch, tmp, terms, spread, slabs, back,
          work_x, inv_x, work_y, inv_y, y_own, y_buf, y_mid, y_buf2,
          rs_send, rs_recv, ag_send, ag_recv, t_send, t_recv,
          y_send, y_recv, y2_send, y2_recv, b_send, b_recv):
    ny, nz, nv, planes, rows_y, rows_z, cells, ranks_x, ranks_y, divisor_x, divisor_y = dims
    members = ny * nz * nv
    inner = nz * nv
    grp = lax.axis_index("grp")
    my_y, my_z, my_v = lax.axis_index("gy"), lax.axis_index("gz"), lax.axis_index("vert")
    my_in = my_z * nv + my_v
    me = my_y * inner + my_in

    def device(y, i):
        return (grp, y, i // nv, lax.rem(i, nv))

    def member(m):
        return device(m // inner, lax.rem(m, inner))

    others = [lax.rem(me + k, members) for k in range(1, members)]
    others_y = [lax.rem(my_y + k, ny) for k in range(1, ny)]
    others_in = [lax.rem(my_in + k, inner) for k in range(1, inner)]

    barrier = pltpu.get_barrier_semaphore()
    for m in others:
        pl.semaphore_signal(barrier, inc=1, device_id=member(m), device_id_type=MESH)

    part[...] = jnp.zeros_like(part)
    omega = omega_x[...]
    chunk = 256
    per_plane = rows_y * rows_z // chunk

    def sketch_step(c, carry):
        block = field[pl.ds(pl.multiple_of(c * chunk, chunk), chunk), :]
        proj = mm(block, omega)
        part[...] += mm(proj.T, block)
        return carry

    lax.fori_loop(0, planes * per_plane, sketch_step, 0)
    pl.semaphore_wait(barrier, members - 1)

    def remote(src, dst, send, recv, target):
        return pltpu.make_async_remote_copy(src_ref=src, dst_ref=dst, send_sem=send, recv_sem=recv,
                                            device_id=target, device_id_type=MESH)

    share = ranks_x // members

    def part_rows(m):
        return pl.ds(pl.multiple_of(m * share, share), share)

    def rs_copy(m, slot):
        return remote(part.at[part_rows(m)], gathered.at[slot], rs_send.at[m], rs_recv.at[slot], member(m))

    for m in others:
        rs_copy(m, me).start()
    gathered[me] = part[part_rows(me), :]
    for m in others:
        rs_copy(m, m).wait_recv()
    total = gathered[0]
    for m in range(1, members):
        total = total + gathered[m]
    total = total / divisor_x
    own_sum[...] = total
    sketch[part_rows(me), :] = total

    def ag_copy(m, slot):
        return remote(own_sum, sketch.at[part_rows(slot)], ag_send.at[m], ag_recv.at[slot], member(m))

    for m in others:
        ag_copy(m, me).start()
    for m in others:
        ag_copy(m, m).wait_recv()

    depth = rows_z // ny
    sketch_t = sketch[...]

    def t_copy(v, y, slot):
        return remote(terms.at[v, pl.ds(pl.multiple_of(y * depth, depth), depth)],
                      spread.at[v, :, pl.ds(pl.multiple_of(slot * rows_y, rows_y), rows_y)],
                      t_send.at[v, y], t_recv.at[v, slot], device(y, my_in))

    for v in range(planes):
        for c in range(per_plane):
            start = (v * per_plane + c) * chunk
            tmp[pl.ds(c * chunk, chunk), :] = mm_nt(field[pl.ds(start, chunk), :], sketch_t)
        for z in range(rows_z):
            terms[v, z] = tmp[pl.ds(z, rows_y, stride=rows_z), :]
        for y in others_y:
            t_copy(v, y, my_y).start()
        spread[v, :, pl.ds(pl.multiple_of(my_y * rows_y, rows_y), rows_y), :] = (
            terms[v, pl.ds(pl.multiple_of(my_y * depth, depth), depth)])

    work_x[...] = mm_nt(sketch_t, sketch_t)
    eliminate(work_x, inv_x, ranks_x)
    kept_x = lax.broadcasted_iota(jnp.int32, (ranks_x, 1), 0) < rank_x[0]
    right = jnp.where(kept_x, inv_x[...], 0.0)
    fx_out[...] = mm(right, sketch_t).T

    all_y = ny * rows_y
    for v in range(planes):
        for y in others_y:
            t_copy(v, y, y).wait_recv()
        block = mm_nt(spread[v].reshape(depth * all_y, ranks_x), right)
        for z in range(depth):
            slabs[:, pl.ds((v * depth + z) * ranks_x, ranks_x)] = block[z * all_y:(z + 1) * all_y, :]
    gram = mm_nt(slabs[...], slabs[...])
    y_own[...] = mm(omega_y_t[...], gram)

    def y_copy(i, slot):
        return remote(y_own, y_buf.at[slot], y_send.at[i], y_recv.at[slot], device(my_y, i))

    for i in others_in:
        y_copy(i, my_in).start()
    y_buf[my_in] = y_own[...]
    for i in others_in:
        y_copy(i, i).wait_recv()
    total = y_buf[0]
    for i in range(1, inner):
        total = total + y_buf[i]
    y_mid[...] = total

    def y2_copy(y, slot):
        return remote(y_mid, y_buf2.at[slot], y2_send.at[y], y2_recv.at[slot], device(y, my_in))

    for y in others_y:
        y2_copy(y, my_y).start()
    y_buf2[my_y] = total
    for y in others_y:
        y2_copy(y, y).wait_recv()
    total = y_buf2[0]
    for y in range(1, ny):
        total = total + y_buf2[y]
    sketch_y_t = total / divisor_y

    work_y[...] = mm_nt(sketch_y_t, sketch_y_t)
    eliminate(work_y, inv_y, ranks_y)
    kept_y = lax.broadcasted_iota(jnp.int32, (ranks_y, 1), 0) < rank_y[0]
    factor_y_t = mm(jnp.where(kept_y, inv_y[...], 0.0), sketch_y_t)
    fy_out[...] = factor_y_t.T

    share_k = ranks_y // ny

    def b_copy(y, slot):
        return remote(back.at[:, pl.ds(pl.multiple_of(y * share_k, share_k), share_k)],
                      core_out.at[:, :, pl.ds(pl.multiple_of(slot * depth, depth), depth)],
                      b_send.at[y], b_recv.at[slot], device(y, my_in))

    for v in range(planes):
        width = depth * ranks_x
        block = mm(factor_y_t, slabs[:, pl.ds(v * width, width)])
        for z in range(depth):
            back[v, :, z, :] = block[:, z * ranks_x:(z + 1) * ranks_x]
    for y in others_y:
        b_copy(y, my_y).start()
    core_out[:, :, pl.ds(pl.multiple_of(my_y * depth, depth), depth), :] = (
        back[:, pl.ds(pl.multiple_of(my_y * share_k, share_k), share_k)])
    for y in others_y:
        b_copy(y, y).wait_recv()

    for m in others:
        rs_copy(m, me).wait_send()
        ag_copy(m, me).wait_send()
    for y in others_y:
        for v in range(planes):
            t_copy(v, y, my_y).wait_send()
        y2_copy(y, my_y).wait_send()
        b_copy(y, my_y).wait_send()
    for i in others_in:
        y_copy(i, my_in).wait_send()


def fused_body(field, omega_x, omega_y, rank_x, rank_y):
    planes, rows_y, rows_z, cells = field.shape
    ny, nz, nv = lax.axis_size("gy"), lax.axis_size("gz"), lax.axis_size("vert")
    ranks_x, ranks_y = omega_x.shape[1], omega_y.shape[1]
    members, inner, depth, all_y = ny * nz * nv, nz * nv, rows_z // ny, rows_y * ny
    divisor_x = float(planes * nv * all_y * rows_z * nz)
    divisor_y = float(planes * nv * rows_z * nz * ranks_x)
    dims = (ny, nz, nv, planes, rows_y, rows_z, cells, ranks_x, ranks_y, divisor_x, divisor_y)
    vmem = pl.BlockSpec(memory_space=pltpu.VMEM)
    smem = pl.BlockSpec(memory_space=pltpu.SMEM)
    dma = pltpu.SemaphoreType.DMA

    def buf(*shape):
        return pltpu.VMEM(shape, jnp.float32)

    def out(*shape):
        return jax.ShapeDtypeStruct(shape, jnp.float32)

    return pl.pallas_call(
        functools.partial(fused, dims),
        out_shape=(out(planes, ranks_y // ny, rows_z * 1, ranks_x), out(cells, ranks_x), out(all_y, ranks_y)),
        in_specs=[smem, smem, vmem, vmem, vmem],
        out_specs=(vmem, vmem, vmem),
        scratch_shapes=[
            buf(ranks_x, cells), buf(members, ranks_x // members, cells), buf(ranks_x // members, cells),
            buf(ranks_x, cells), buf(rows_y * rows_z, ranks_x), buf(planes, rows_z, rows_y, ranks_x),
            buf(planes, depth, all_y, ranks_x), buf(all_y, planes * depth * ranks_x),
            buf(planes, ranks_y, depth, ranks_x),
            buf(ranks_x, ranks_x), buf(ranks_x, ranks_x), buf(ranks_y, ranks_y), buf(ranks_y, ranks_y),
            buf(ranks_y, all_y), buf(inner, ranks_y, all_y), buf(ranks_y, all_y), buf(ny, ranks_y, all_y),
            dma((members,)), dma((members,)), dma((members,)), dma((members,)),
            dma((planes, ny)), dma((planes, ny)),
            dma((inner,)), dma((inner,)), dma((ny,)), dma((ny,)), dma((ny,)), dma((ny,)),
        ],
        compiler_params=pltpu.CompilerParams(collective_id=0, has_side_effects=True,
                                             vmem_limit_bytes=40 * 1024 * 1024),
    )(rank_x, rank_y, field.reshape(-1, cells), omega_x, omega_y.T)


def solution(mesh):
    in_specs = (P(("grp", "vert"), "gy", "gz", None), P(), P(), P("grp"), P("grp"))
    out_specs = (P(("grp", "vert"), "gy", "gz", None), P("grp", None), P("grp", None))
    members = mesh.shape["gy"] * mesh.shape["gz"] * mesh.shape["vert"]
    body = fused_body if members <= 16 and mesh.shape["gy"] <= 4 else plain_body
    return jax.shard_map(body, mesh=mesh, in_specs=in_specs, out_specs=out_specs, check_vma=False)
```

```python
import functools

import jax
import jax.numpy as jnp
from jax import lax
from jax.experimental import pallas as pl
from jax.experimental.pallas import tpu as pltpu
from jax.sharding import PartitionSpec as P

HIGHEST = lax.Precision.HIGHEST


def inverse_factor(sketch):
    small_gram = jnp.dot(sketch.T, sketch, precision=HIGHEST)
    lower = jnp.linalg.cholesky(small_gram)
    eye = jnp.eye(lower.shape[0], dtype=jnp.float32)
    return lax.linalg.triangular_solve(lower, eye, left_side=True, lower=True)


def plain_body(field, omega_x, omega_y, rank_x, rank_y):
    planes, rows_y, rows_z, cells_x = field.shape
    all_planes = planes * lax.axis_size("vert")
    all_rows_y = rows_y * lax.axis_size("gy")
    all_rows_z = rows_z * lax.axis_size("gz")
    flat = field.reshape(-1, cells_x)
    proj = jnp.dot(flat, omega_x, precision=HIGHEST)
    local_sketch = jnp.dot(flat.T, proj, precision=HIGHEST)
    sketch_x = lax.psum(local_sketch, ("gy", "gz", "vert")) / float(all_planes * all_rows_y * all_rows_z)
    ranks_x = sketch_x.shape[1]
    terms = jnp.dot(flat, sketch_x, precision=HIGHEST).reshape(planes, rows_y, rows_z, ranks_x)
    spread = lax.all_to_all(terms, "gy", split_axis=2, concat_axis=1, tiled=True)
    inv_x = inverse_factor(sketch_x)
    kept_x = (jnp.arange(ranks_x) < rank_x[0]).astype(jnp.float32)
    inv_x = inv_x * kept_x[:, None]
    factor_x = jnp.dot(sketch_x, inv_x.T, precision=HIGHEST)
    core_x = jnp.einsum("vyzr,sr->vyzs", spread, inv_x, precision=HIGHEST)
    divisor_y = float(all_planes * all_rows_z * ranks_x)
    local_gram_y = jnp.einsum("vazr,vbzr->ab", core_x, core_x, precision=HIGHEST)
    sketch_y = lax.psum(jnp.dot(local_gram_y, omega_y, precision=HIGHEST), ("gy", "gz", "vert")) / divisor_y
    inv_y = inverse_factor(sketch_y)
    kept_y = (jnp.arange(inv_y.shape[0]) < rank_y[0]).astype(jnp.float32)
    factor_y = jnp.dot(sketch_y, (inv_y * kept_y[:, None]).T, precision=HIGHEST)
    mine = jnp.einsum("vyzr,yk->vkzr", core_x, factor_y, precision=HIGHEST)
    core = lax.all_to_all(mine, "gy", split_axis=1, concat_axis=2, tiled=True)
    return (core, factor_x, factor_y)


MESH = pl.DeviceIdType.MESH
NT = (((1,), (1,)), ((), ()))


def mm(a, b):
    return jnp.dot(a, b, precision=HIGHEST, preferred_element_type=jnp.float32)


def mm_nt(a, b):
    return lax.dot_general(a, b, NT, precision=HIGHEST, preferred_element_type=jnp.float32)


def split(x):
    high = x.astype(jnp.bfloat16)
    return high, (x - high.astype(jnp.float32)).astype(jnp.bfloat16)


def mm3(a, b, dims=(((1,), (0,)), ((), ()))):
    def one(x, y):
        return lax.dot_general(x, y, dims, preferred_element_type=jnp.float32)

    return one(a[0], b[0]) + (one(a[0], b[1]) + one(a[1], b[0]))


def eliminate(work, inv, size):
    rows = lax.broadcasted_iota(jnp.int32, (size, size), 0)
    cols = lax.broadcasted_iota(jnp.int32, (size, size), 1)
    inv[...] = (rows == cols).astype(jnp.float32)
    row_ids = lax.broadcasted_iota(jnp.int32, (size, 1), 0)
    lane_ids = lax.broadcasted_iota(jnp.int32, (1, size), 1)

    def step(j, pivots):
        full = work[...]
        row = work[pl.ds(j, 1), :]
        column = jnp.sum(jnp.where(cols == j, full, 0.0), axis=1, keepdims=True)
        pivot = jnp.sum(jnp.where(lane_ids == j, row, 0.0), axis=1, keepdims=True)
        factor = jnp.where(row_ids > j, column / pivot, 0.0)
        inv_row = inv[pl.ds(j, 1), :]
        work[...] = full - factor * row
        inv[...] = inv[...] - factor * inv_row
        return jnp.where(row_ids == j, pivot, pivots)

    pivots = lax.fori_loop(0, size, step, jnp.ones((size, 1), jnp.float32))
    inv[...] = inv[...] * lax.rsqrt(pivots)


def fused(dims, rank_x, rank_y, field, omega_x, omega_y_t, core_out, fx_out, fy_out,
          part, gathered, own_sum, sketch, tmp, terms, spread, slabs, back,
          work_x, inv_x, work_y, inv_y, y_own, y_buf, y_mid, y_buf2,
          rs_send, rs_recv, ag_send, ag_recv, t_send, t_recv,
          y_send, y_recv, y2_send, y2_recv, b_send, b_recv):
    ny, nz, nv, planes, rows_y, rows_z, cells, ranks_x, ranks_y, divisor_x, divisor_y = dims
    members = ny * nz * nv
    inner = nz * nv
    grp = lax.axis_index("grp")
    my_y, my_z, my_v = lax.axis_index("gy"), lax.axis_index("gz"), lax.axis_index("vert")
    my_in = my_z * nv + my_v
    me = my_y * inner + my_in

    def device(y, i):
        return (grp, y, i // nv, lax.rem(i, nv))

    def member(m):
        return device(m // inner, lax.rem(m, inner))

    others = [lax.rem(me + k, members) for k in range(1, members)]
    others_y = [lax.rem(my_y + k, ny) for k in range(1, ny)]
    others_in = [lax.rem(my_in + k, inner) for k in range(1, inner)]

    barrier = pltpu.get_barrier_semaphore()
    for m in others:
        pl.semaphore_signal(barrier, inc=1, device_id=member(m), device_id_type=MESH)

    part[...] = jnp.zeros_like(part)
    omega = split(omega_x[...])
    chunk = 256
    per_plane = rows_y * rows_z // chunk

    def sketch_step(c, carry):
        block = split(field[pl.ds(pl.multiple_of(c * chunk, chunk), chunk), :])
        proj = mm3(block, omega)
        part[...] += mm3(split(proj.T), block)
        return carry

    lax.fori_loop(0, planes * per_plane, sketch_step, 0)
    pl.semaphore_wait(barrier, members - 1)

    def remote(src, dst, send, recv, target):
        return pltpu.make_async_remote_copy(src_ref=src, dst_ref=dst, send_sem=send, recv_sem=recv,
                                            device_id=target, device_id_type=MESH)

    share = ranks_x // members

    def part_rows(m):
        return pl.ds(pl.multiple_of(m * share, share), share)

    def rs_copy(m, slot):
        return remote(part.at[part_rows(m)], gathered.at[slot], rs_send.at[m], rs_recv.at[slot], member(m))

    for m in others:
        rs_copy(m, me).start()
    gathered[me] = part[part_rows(me), :]
    for m in others:
        rs_copy(m, m).wait_recv()
    total = gathered[0]
    for m in range(1, members):
        total = total + gathered[m]
    total = total / divisor_x
    own_sum[...] = total
    sketch[part_rows(me), :] = total

    def ag_copy(m, slot):
        return remote(own_sum, sketch.at[part_rows(slot)], ag_send.at[m], ag_recv.at[slot], member(m))

    for m in others:
        ag_copy(m, me).start()
    for m in others:
        ag_copy(m, m).wait_recv()

    depth = rows_z // ny
    sketch_t = sketch[...]
    sketch_parts = split(sketch_t)

    def t_copy(v, y, slot):
        return remote(terms.at[v, pl.ds(pl.multiple_of(y * depth, depth), depth)],
                      spread.at[v, :, pl.ds(pl.multiple_of(slot * rows_y, rows_y), rows_y)],
                      t_send.at[v, y], t_recv.at[v, slot], device(y, my_in))

    for v in range(planes):
        for c in range(per_plane):
            start = (v * per_plane + c) * chunk
            tmp[pl.ds(c * chunk, chunk), :] = mm3(split(field[pl.ds(start, chunk), :]), sketch_parts, NT)
        for z in range(rows_z):
            terms[v, z] = tmp[pl.ds(z, rows_y, stride=rows_z), :]
        for y in others_y:
            t_copy(v, y, my_y).start()
        spread[v, :, pl.ds(pl.multiple_of(my_y * rows_y, rows_y), rows_y), :] = (
            terms[v, pl.ds(pl.multiple_of(my_y * depth, depth), depth)])

    work_x[...] = mm_nt(sketch_t, sketch_t)
    eliminate(work_x, inv_x, ranks_x)
    kept_x = lax.broadcasted_iota(jnp.int32, (ranks_x, 1), 0) < rank_x[0]
    right = jnp.where(kept_x, inv_x[...], 0.0)
    fx_out[...] = mm(right, sketch_t).T

    all_y = ny * rows_y
    for v in range(planes):
        for y in others_y:
            t_copy(v, y, y).wait_recv()
        block = mm_nt(spread[v].reshape(depth * all_y, ranks_x), right)
        for z in range(depth):
            slabs[:, pl.ds((v * depth + z) * ranks_x, ranks_x)] = block[z * all_y:(z + 1) * all_y, :]
    gram = mm_nt(slabs[...], slabs[...])
    y_own[...] = mm(omega_y_t[...], gram)

    def y_copy(i, slot):
        return remote(y_own, y_buf.at[slot], y_send.at[i], y_recv.at[slot], device(my_y, i))

    for i in others_in:
        y_copy(i, my_in).start()
    y_buf[my_in] = y_own[...]
    for i in others_in:
        y_copy(i, i).wait_recv()
    total = y_buf[0]
    for i in range(1, inner):
        total = total + y_buf[i]
    y_mid[...] = total

    def y2_copy(y, slot):
        return remote(y_mid, y_buf2.at[slot], y2_send.at[y], y2_recv.at[slot], device(y, my_in))

    for y in others_y:
        y2_copy(y, my_y).start()
    y_buf2[my_y] = total
    for y in others_y:
        y2_copy(y, y).wait_recv()
    total = y_buf2[0]
    for y in range(1, ny):
        total = total + y_buf2[y]
    sketch_y_t = total / divisor_y

    work_y[...] = mm_nt(sketch_y_t, sketch_y_t)
    eliminate(work_y, inv_y, ranks_y)
    kept_y = lax.broadcasted_iota(jnp.int32, (ranks_y, 1), 0) < rank_y[0]
    factor_y_t = mm(jnp.where(kept_y, inv_y[...], 0.0), sketch_y_t)
    fy_out[...] = factor_y_t.T

    share_k = ranks_y // ny

    def b_copy(y, slot):
        return remote(back.at[:, pl.ds(pl.multiple_of(y * share_k, share_k), share_k)],
                      core_out.at[:, :, pl.ds(pl.multiple_of(slot * depth, depth), depth)],
                      b_send.at[y], b_recv.at[slot], device(y, my_in))

    for v in range(planes):
        width = depth * ranks_x
        block = mm(factor_y_t, slabs[:, pl.ds(v * width, width)])
        for z in range(depth):
            back[v, :, z, :] = block[:, z * ranks_x:(z + 1) * ranks_x]
    for y in others_y:
        b_copy(y, my_y).start()
    core_out[:, :, pl.ds(pl.multiple_of(my_y * depth, depth), depth), :] = (
        back[:, pl.ds(pl.multiple_of(my_y * share_k, share_k), share_k)])
    for y in others_y:
        b_copy(y, y).wait_recv()

    for m in others:
        rs_copy(m, me).wait_send()
        ag_copy(m, me).wait_send()
    for y in others_y:
        for v in range(planes):
            t_copy(v, y, my_y).wait_send()
        y2_copy(y, my_y).wait_send()
        b_copy(y, my_y).wait_send()
    for i in others_in:
        y_copy(i, my_in).wait_send()


def fused_body(field, omega_x, omega_y, rank_x, rank_y):
    planes, rows_y, rows_z, cells = field.shape
    ny, nz, nv = lax.axis_size("gy"), lax.axis_size("gz"), lax.axis_size("vert")
    ranks_x, ranks_y = omega_x.shape[1], omega_y.shape[1]
    members, inner, depth, all_y = ny * nz * nv, nz * nv, rows_z // ny, rows_y * ny
    divisor_x = float(planes * nv * all_y * rows_z * nz)
    divisor_y = float(planes * nv * rows_z * nz * ranks_x)
    dims = (ny, nz, nv, planes, rows_y, rows_z, cells, ranks_x, ranks_y, divisor_x, divisor_y)
    vmem = pl.BlockSpec(memory_space=pltpu.VMEM)
    smem = pl.BlockSpec(memory_space=pltpu.SMEM)
    dma = pltpu.SemaphoreType.DMA

    def buf(*shape):
        return pltpu.VMEM(shape, jnp.float32)

    def out(*shape):
        return jax.ShapeDtypeStruct(shape, jnp.float32)

    return pl.pallas_call(
        functools.partial(fused, dims),
        out_shape=(out(planes, ranks_y // ny, rows_z * 1, ranks_x), out(cells, ranks_x), out(all_y, ranks_y)),
        in_specs=[smem, smem, vmem, vmem, vmem],
        out_specs=(vmem, vmem, vmem),
        scratch_shapes=[
            buf(ranks_x, cells), buf(members, ranks_x // members, cells), buf(ranks_x // members, cells),
            buf(ranks_x, cells), buf(rows_y * rows_z, ranks_x), buf(planes, rows_z, rows_y, ranks_x),
            buf(planes, depth, all_y, ranks_x), buf(all_y, planes * depth * ranks_x),
            buf(planes, ranks_y, depth, ranks_x),
            buf(ranks_x, ranks_x), buf(ranks_x, ranks_x), buf(ranks_y, ranks_y), buf(ranks_y, ranks_y),
            buf(ranks_y, all_y), buf(inner, ranks_y, all_y), buf(ranks_y, all_y), buf(ny, ranks_y, all_y),
            dma((members,)), dma((members,)), dma((members,)), dma((members,)),
            dma((planes, ny)), dma((planes, ny)),
            dma((inner,)), dma((inner,)), dma((ny,)), dma((ny,)), dma((ny,)), dma((ny,)),
        ],
        compiler_params=pltpu.CompilerParams(collective_id=0, has_side_effects=True,
                                             vmem_limit_bytes=40 * 1024 * 1024),
    )(rank_x, rank_y, field.reshape(-1, cells), omega_x, omega_y.T)


def solution(mesh):
    in_specs = (P(("grp", "vert"), "gy", "gz", None), P(), P(), P("grp"), P("grp"))
    out_specs = (P(("grp", "vert"), "gy", "gz", None), P("grp", None), P("grp", None))
    members = mesh.shape["gy"] * mesh.shape["gz"] * mesh.shape["vert"]
    body = fused_body if members <= 16 and mesh.shape["gy"] <= 4 else plain_body
    return jax.shard_map(body, mesh=mesh, in_specs=in_specs, out_specs=out_specs, check_vma=False)
```

```python
import functools

import jax
import jax.numpy as jnp
from jax import lax
from jax.experimental import pallas as pl
from jax.experimental.pallas import tpu as pltpu
from jax.sharding import PartitionSpec as P

HIGHEST = lax.Precision.HIGHEST


def inverse_factor(sketch):
    small_gram = jnp.dot(sketch.T, sketch, precision=HIGHEST)
    lower = jnp.linalg.cholesky(small_gram)
    eye = jnp.eye(lower.shape[0], dtype=jnp.float32)
    return lax.linalg.triangular_solve(lower, eye, left_side=True, lower=True)


def plain_body(field, omega_x, omega_y, rank_x, rank_y):
    planes, rows_y, rows_z, cells_x = field.shape
    all_planes = planes * lax.axis_size("vert")
    all_rows_y = rows_y * lax.axis_size("gy")
    all_rows_z = rows_z * lax.axis_size("gz")
    flat = field.reshape(-1, cells_x)
    proj = jnp.dot(flat, omega_x, precision=HIGHEST)
    local_sketch = jnp.dot(flat.T, proj, precision=HIGHEST)
    sketch_x = lax.psum(local_sketch, ("gy", "gz", "vert")) / float(all_planes * all_rows_y * all_rows_z)
    ranks_x = sketch_x.shape[1]
    terms = jnp.dot(flat, sketch_x, precision=HIGHEST).reshape(planes, rows_y, rows_z, ranks_x)
    spread = lax.all_to_all(terms, "gy", split_axis=2, concat_axis=1, tiled=True)
    inv_x = inverse_factor(sketch_x)
    kept_x = (jnp.arange(ranks_x) < rank_x[0]).astype(jnp.float32)
    inv_x = inv_x * kept_x[:, None]
    factor_x = jnp.dot(sketch_x, inv_x.T, precision=HIGHEST)
    core_x = jnp.einsum("vyzr,sr->vyzs", spread, inv_x, precision=HIGHEST)
    divisor_y = float(all_planes * all_rows_z * ranks_x)
    local_gram_y = jnp.einsum("vazr,vbzr->ab", core_x, core_x, precision=HIGHEST)
    sketch_y = lax.psum(jnp.dot(local_gram_y, omega_y, precision=HIGHEST), ("gy", "gz", "vert")) / divisor_y
    inv_y = inverse_factor(sketch_y)
    kept_y = (jnp.arange(inv_y.shape[0]) < rank_y[0]).astype(jnp.float32)
    factor_y = jnp.dot(sketch_y, (inv_y * kept_y[:, None]).T, precision=HIGHEST)
    mine = jnp.einsum("vyzr,yk->vkzr", core_x, factor_y, precision=HIGHEST)
    core = lax.all_to_all(mine, "gy", split_axis=1, concat_axis=2, tiled=True)
    return (core, factor_x, factor_y)


MESH = pl.DeviceIdType.MESH
NT = (((1,), (1,)), ((), ()))


def mm(a, b):
    return jnp.dot(a, b, precision=HIGHEST, preferred_element_type=jnp.float32)


def mm_nt(a, b):
    return lax.dot_general(a, b, NT, precision=HIGHEST, preferred_element_type=jnp.float32)


def split(a):
    high = a.astype(jnp.bfloat16)
    return high, (a - high.astype(jnp.float32)).astype(jnp.bfloat16)


def mm_split(a, b, dims=(((1,), (0,)), ((), ()))):
    def dot(x, y):
        return lax.dot_general(x, y, dims, preferred_element_type=jnp.float32)

    return dot(a[0], b[0]) + (dot(a[0], b[1]) + dot(a[1], b[0]))


def eliminate(work, inv, size):
    rows = lax.broadcasted_iota(jnp.int32, (size, size), 0)
    cols = lax.broadcasted_iota(jnp.int32, (size, size), 1)
    inv[...] = (rows == cols).astype(jnp.float32)
    row_ids = lax.broadcasted_iota(jnp.int32, (size, 1), 0)
    lane_ids = lax.broadcasted_iota(jnp.int32, (1, size), 1)

    def step(j, pivots):
        full = work[...]
        row = work[pl.ds(j, 1), :]
        column = jnp.sum(jnp.where(cols == j, full, 0.0), axis=1, keepdims=True)
        pivot = jnp.sum(jnp.where(lane_ids == j, row, 0.0), axis=1, keepdims=True)
        factor = jnp.where(row_ids > j, column * (1.0 / pivot), 0.0)
        inv_row = inv[pl.ds(j, 1), :]
        work[...] = full - factor * row
        inv[...] = inv[...] - factor * inv_row
        return jnp.where(row_ids == j, pivot, pivots)

    pivots = lax.fori_loop(0, size, step, jnp.ones((size, 1), jnp.float32))
    inv[...] = inv[...] * lax.rsqrt(pivots)


def fused(dims, rank_x, rank_y, field, omega_x, omega_y_t, core_out, fx_out, fy_out,
          part, gathered, own_sum, sketch, tmp, terms, spread, slabs, back,
          work_x, inv_x, work_y, inv_y, y_own, y_buf, y_mid, y_buf2,
          rs_send, rs_recv, ag_send, ag_recv, t_send, t_recv,
          y_send, y_recv, y2_send, y2_recv, b_send, b_recv):
    ny, nz, nv, planes, rows_y, rows_z, cells, ranks_x, ranks_y, divisor_x, divisor_y = dims
    members = ny * nz * nv
    inner = nz * nv
    grp = lax.axis_index("grp")
    my_y, my_z, my_v = lax.axis_index("gy"), lax.axis_index("gz"), lax.axis_index("vert")
    my_in = my_z * nv + my_v
    me = my_y * inner + my_in

    def device(y, i):
        return (grp, y, i // nv, lax.rem(i, nv))

    def member(m):
        return device(m // inner, lax.rem(m, inner))

    others = [lax.rem(me + k, members) for k in range(1, members)]
    others_y = [lax.rem(my_y + k, ny) for k in range(1, ny)]
    others_in = [lax.rem(my_in + k, inner) for k in range(1, inner)]

    barrier = pltpu.get_barrier_semaphore()
    for m in others:
        pl.semaphore_signal(barrier, inc=1, device_id=member(m), device_id_type=MESH)

    part[...] = jnp.zeros_like(part)
    omega = split(omega_x[...])
    chunk = 256
    per_plane = rows_y * rows_z // chunk

    def sketch_step(c, carry):
        block = split(field[pl.ds(pl.multiple_of(c * chunk, chunk), chunk), :])
        proj = mm_split(block, omega)
        part[...] += mm_split(split(proj.T), block)
        return carry

    lax.fori_loop(0, planes * per_plane, sketch_step, 0)
    pl.semaphore_wait(barrier, members - 1)

    def remote(src, dst, send, recv, target):
        return pltpu.make_async_remote_copy(src_ref=src, dst_ref=dst, send_sem=send, recv_sem=recv,
                                            device_id=target, device_id_type=MESH)

    share = ranks_x // members

    def part_rows(m):
        return pl.ds(pl.multiple_of(m * share, share), share)

    def rs_copy(m, slot):
        return remote(part.at[part_rows(m)], gathered.at[slot], rs_send.at[m], rs_recv.at[slot], member(m))

    for m in others:
        rs_copy(m, me).start()
    gathered[me] = part[part_rows(me), :]
    for m in others:
        rs_copy(m, m).wait_recv()
    total = gathered[0]
    for m in range(1, members):
        total = total + gathered[m]
    total = total / divisor_x
    own_sum[...] = total
    sketch[part_rows(me), :] = total

    def ag_copy(m, slot):
        return remote(own_sum, sketch.at[part_rows(slot)], ag_send.at[m], ag_recv.at[slot], member(m))

    for m in others:
        ag_copy(m, me).start()
    for m in others:
        ag_copy(m, m).wait_recv()

    depth = rows_z // ny
    sketch_t = sketch[...]
    sketch_parts = split(sketch_t)

    def t_copy(v, y, slot):
        return remote(terms.at[v, pl.ds(pl.multiple_of(y * depth, depth), depth)],
                      spread.at[v, :, pl.ds(pl.multiple_of(slot * rows_y, rows_y), rows_y)],
                      t_send.at[v, y], t_recv.at[v, slot], device(y, my_in))

    for v in range(planes):
        for c in range(per_plane):
            start = (v * per_plane + c) * chunk
            tmp[pl.ds(c * chunk, chunk), :] = mm_split(split(field[pl.ds(start, chunk), :]), sketch_parts, NT)
        for z in range(rows_z):
            terms[v, z] = tmp[pl.ds(z, rows_y, stride=rows_z), :]
        for y in others_y:
            t_copy(v, y, my_y).start()
        spread[v, :, pl.ds(pl.multiple_of(my_y * rows_y, rows_y), rows_y), :] = (
            terms[v, pl.ds(pl.multiple_of(my_y * depth, depth), depth)])

    work_x[...] = mm_nt(sketch_t, sketch_t)
    eliminate(work_x, inv_x, ranks_x)
    kept_x = lax.broadcasted_iota(jnp.int32, (ranks_x, 1), 0) < rank_x[0]
    right = jnp.where(kept_x, inv_x[...], 0.0)
    fx_out[...] = mm(right, sketch_t).T

    all_y = ny * rows_y
    for v in range(planes):
        for y in others_y:
            t_copy(v, y, y).wait_recv()
        block = mm_nt(spread[v].reshape(depth * all_y, ranks_x), right)
        for z in range(depth):
            slabs[:, pl.ds((v * depth + z) * ranks_x, ranks_x)] = block[z * all_y:(z + 1) * all_y, :]
    gram = mm_nt(slabs[...], slabs[...])
    y_own[...] = mm(omega_y_t[...], gram)

    def y_copy(i, slot):
        return remote(y_own, y_buf.at[slot], y_send.at[i], y_recv.at[slot], device(my_y, i))

    for i in others_in:
        y_copy(i, my_in).start()
    y_buf[my_in] = y_own[...]
    for i in others_in:
        y_copy(i, i).wait_recv()
    total = y_buf[0]
    for i in range(1, inner):
        total = total + y_buf[i]
    y_mid[...] = total

    def y2_copy(y, slot):
        return remote(y_mid, y_buf2.at[slot], y2_send.at[y], y2_recv.at[slot], device(y, my_in))

    for y in others_y:
        y2_copy(y, my_y).start()
    y_buf2[my_y] = total
    for y in others_y:
        y2_copy(y, y).wait_recv()
    total = y_buf2[0]
    for y in range(1, ny):
        total = total + y_buf2[y]
    sketch_y_t = total / divisor_y

    work_y[...] = mm_nt(sketch_y_t, sketch_y_t)
    eliminate(work_y, inv_y, ranks_y)
    kept_y = lax.broadcasted_iota(jnp.int32, (ranks_y, 1), 0) < rank_y[0]
    factor_y_t = mm(jnp.where(kept_y, inv_y[...], 0.0), sketch_y_t)
    fy_out[...] = factor_y_t.T

    share_k = ranks_y // ny

    def b_copy(y, slot):
        return remote(back.at[:, pl.ds(pl.multiple_of(y * share_k, share_k), share_k)],
                      core_out.at[:, :, pl.ds(pl.multiple_of(slot * depth, depth), depth)],
                      b_send.at[y], b_recv.at[slot], device(y, my_in))

    for v in range(planes):
        width = depth * ranks_x
        block = mm(factor_y_t, slabs[:, pl.ds(v * width, width)])
        for z in range(depth):
            back[v, :, z, :] = block[:, z * ranks_x:(z + 1) * ranks_x]
    for y in others_y:
        b_copy(y, my_y).start()
    core_out[:, :, pl.ds(pl.multiple_of(my_y * depth, depth), depth), :] = (
        back[:, pl.ds(pl.multiple_of(my_y * share_k, share_k), share_k)])
    for y in others_y:
        b_copy(y, y).wait_recv()

    for m in others:
        rs_copy(m, me).wait_send()
        ag_copy(m, me).wait_send()
    for y in others_y:
        for v in range(planes):
            t_copy(v, y, my_y).wait_send()
        y2_copy(y, my_y).wait_send()
        b_copy(y, my_y).wait_send()
    for i in others_in:
        y_copy(i, my_in).wait_send()


def fused_body(field, omega_x, omega_y, rank_x, rank_y):
    planes, rows_y, rows_z, cells = field.shape
    ny, nz, nv = lax.axis_size("gy"), lax.axis_size("gz"), lax.axis_size("vert")
    ranks_x, ranks_y = omega_x.shape[1], omega_y.shape[1]
    members, inner, depth, all_y = ny * nz * nv, nz * nv, rows_z // ny, rows_y * ny
    divisor_x = float(planes * nv * all_y * rows_z * nz)
    divisor_y = float(planes * nv * rows_z * nz * ranks_x)
    dims = (ny, nz, nv, planes, rows_y, rows_z, cells, ranks_x, ranks_y, divisor_x, divisor_y)
    vmem = pl.BlockSpec(memory_space=pltpu.VMEM)
    smem = pl.BlockSpec(memory_space=pltpu.SMEM)
    dma = pltpu.SemaphoreType.DMA

    def buf(*shape):
        return pltpu.VMEM(shape, jnp.float32)

    def out(*shape):
        return jax.ShapeDtypeStruct(shape, jnp.float32)

    return pl.pallas_call(
        functools.partial(fused, dims),
        out_shape=(out(planes, ranks_y // ny, rows_z * 1, ranks_x), out(cells, ranks_x), out(all_y, ranks_y)),
        in_specs=[smem, smem, vmem, vmem, vmem],
        out_specs=(vmem, vmem, vmem),
        scratch_shapes=[
            buf(ranks_x, cells), buf(members, ranks_x // members, cells), buf(ranks_x // members, cells),
            buf(ranks_x, cells), buf(rows_y * rows_z, ranks_x), buf(planes, rows_z, rows_y, ranks_x),
            buf(planes, depth, all_y, ranks_x), buf(all_y, planes * depth * ranks_x),
            buf(planes, ranks_y, depth, ranks_x),
            buf(ranks_x, ranks_x), buf(ranks_x, ranks_x), buf(ranks_y, ranks_y), buf(ranks_y, ranks_y),
            buf(ranks_y, all_y), buf(inner, ranks_y, all_y), buf(ranks_y, all_y), buf(ny, ranks_y, all_y),
            dma((members,)), dma((members,)), dma((members,)), dma((members,)),
            dma((planes, ny)), dma((planes, ny)),
            dma((inner,)), dma((inner,)), dma((ny,)), dma((ny,)), dma((ny,)), dma((ny,)),
        ],
        compiler_params=pltpu.CompilerParams(collective_id=0, has_side_effects=True,
                                             vmem_limit_bytes=40 * 1024 * 1024),
    )(rank_x, rank_y, field.reshape(-1, cells), omega_x, omega_y.T)


def solution(mesh):
    in_specs = (P(("grp", "vert"), "gy", "gz", None), P(), P(), P("grp"), P("grp"))
    out_specs = (P(("grp", "vert"), "gy", "gz", None), P("grp", None), P("grp", None))
    members = mesh.shape["gy"] * mesh.shape["gz"] * mesh.shape["vert"]
    body = fused_body if members <= 16 and mesh.shape["gy"] <= 4 else plain_body
    return jax.shard_map(body, mesh=mesh, in_specs=in_specs, out_specs=out_specs, check_vma=False)
```
